256 devices in a mesh: dp: 64 (over z, y, core), mp: 4 (over x).
Axes of the slice: x: 4, y: 4, z: 8, core: 2. Of those that a mesh axis runs over, the one named last changes fastest.
Arguments:
- grads: bfloat16 [4, 32, 1024, 1024], P('mp', None, 'dp')
- momentum: float32 [4, 32, 1024, 1024], P('mp', None, 'dp'), may hold values from -6 to 6
- root_factors: float32 [4, 64, 1024, 1024], P('mp', 'dp'), as said below
- owner_table: int32 [4, 32], P('mp'), may hold values from 0 to 31, each once within a row
Outputs:
- new_momentum: float32 [4, 32, 1024, 1024], P('mp', None, 'dp')
- direction: bfloat16 [4, 32, 1024, 1024], P('mp', None, 'dp')
The draws below stay inside these ranges and needn't reach their ends.
Inputs may be any that keep to these rules, and one draw needn't show every extreme that they name: `owner_table`: each row names each of the 32 factor pairs once. `root_factors`: each slot holds a symmetric positive definite matrix.
All inputs are finite; a program needn't handle non-finite values.
Results may differ from the reference program's by a relative error of at most 0.0006.
Values may be sent and summed in bfloat16 or wider, within the bound.
A program may use at most 64 MiB of HBM per device.

```python
import math
import jax
import jax.numpy as jnp
from jax import lax

B = 1024
PIECES = 4
BLOCKS = 32
SLOTS = 64


def common_vector(key):
    return jax.random.normal(jax.random.fold_in(key, 77), (B,), jnp.float32)


def draw_grads(key, part):
    shared = common_vector(key)
    key = jax.random.fold_in(key, 11)
    key_base = jax.random.fold_in(key, 0)
    key_rows = jax.random.fold_in(key, 1)
    key_cols = jax.random.fold_in(key, 2)
    key_weights = jax.random.fold_in(key, 4)
    full_shape = (PIECES, BLOCKS, B, B)
    low_log = math.log(0.3)
    high_log = math.log(3.0)
    row_log = jax.random.uniform(key_rows, (PIECES, BLOCKS, B, 1), jnp.float32, low_log, high_log)
    col_log = jax.random.uniform(key_cols, (PIECES, BLOCKS, 1, B), jnp.float32, low_log, high_log)
    rise_factor = jnp.sqrt(1.0 + 2.0 * jnp.arange(B, dtype=jnp.float32) / B).reshape(1, 1, B, 1)
    row_weights = jax.random.normal(key_weights, (PIECES, BLOCKS, B, 1), jnp.float32)
    base_draw = jax.random.normal(key_base, full_shape, jnp.float32)
    base_draw = base_draw + 0.6 * row_weights * shared.reshape(1, 1, 1, B)
    return (base_draw * jnp.exp(row_log + col_log) * rise_factor).astype(jnp.bfloat16)


def draw_root_factors(key, part):
    shared = common_vector(key)
    key = jax.random.fold_in(key, 23)
    key_noise, key_diag, key_strength = jax.random.split(key, 3)
    noise_draw = jax.random.normal(key_noise, (PIECES, SLOTS, B, B), jnp.float32)
    symmetric = (noise_draw + jnp.swapaxes(noise_draw, -1, -2)) * (0.35 / math.sqrt(2.0 * B))
    diagonal = jax.random.uniform(key_diag, (PIECES, SLOTS, 1, B), jnp.float32, 1.0, 2.0)
    strength = jax.random.uniform(key_strength, (PIECES, SLOTS, 1, 1), jnp.float32, 1.0, 2.0)
    aligned = strength * (shared[:, None] * shared[None, :]).reshape(1, 1, B, B) / B
    identity = jnp.eye(B, dtype=jnp.float32)
    return symmetric + identity * diagonal + aligned


def block_scale(key, dims, cuts, low, top_value):
    gain = 1.0
    for axis_at, blocks in cuts:
        heights = jax.random.uniform(jax.random.fold_in(jax.random.fold_in(key, 6), axis_at), (blocks,), jnp.float32, low / len(cuts), top_value / len(cuts))
        gain = gain * jnp.repeat(jnp.exp(heights), dims[axis_at] // blocks).reshape((-1,) + (1,) * (len(dims) - 1 - axis_at))
    return gain


def bell_draw(key, shape, deviation, limit, shards=(), kind=jnp.bfloat16):
    result = deviation * jax.random.normal(key, shape, jnp.float32)
    if shards:
        result = result * block_scale(key, shape, shards, -0.22, 0.18)
    return jnp.clip(result, -limit, limit).astype(kind)


def setup_inputs(seed: int = 0) -> dict:
    arg_keys = jax.random.split(jax.random.key(seed), 5)
    return {
        "grads": draw_grads(jax.random.fold_in(arg_keys[4], 71), 0),
        "momentum": bell_draw(arg_keys[1], (PIECES, BLOCKS, B, B), 1.0, 6.0, ((0, 4), (2, 64)), jnp.float32),
        "root_factors": draw_root_factors(jax.random.fold_in(arg_keys[4], 71), 0),
        "owner_table": jax.vmap(lambda own: jax.random.permutation(own, BLOCKS))(jax.random.split(arg_keys[3], PIECES)).reshape((PIECES, BLOCKS)).astype(jnp.int32),
    }


def matmul_f32(first_matrix, second_matrix):
    return jnp.dot(first_matrix, second_matrix, precision=lax.Precision.HIGHEST)

def reference(grads, momentum, root_factors, owner_table):

    def one_piece(inputs):
        grad_piece, factor_piece, pair_piece = inputs

        def one_block(pair_inputs):
            grad_block, block_pair = pair_inputs
            left_factor = lax.dynamic_index_in_dim(factor_piece, 2 * block_pair, 0, keepdims=False)
            right_factor = lax.dynamic_index_in_dim(factor_piece, 2 * block_pair + 1, 0, keepdims=False)
            grad_float = grad_block.astype(jnp.float32)
            return matmul_f32(matmul_f32(left_factor, grad_float), right_factor)
        return lax.map(one_block, (grad_piece, pair_piece))
    precond = lax.map(one_piece, (grads, root_factors, owner_table))
    grad_sq = lax.optimization_barrier(jnp.sum(jnp.square(grads.astype(jnp.float32)), axis=(0, 2, 3)))
    pre_sq = lax.optimization_barrier(jnp.sum(jnp.square(precond), axis=(0, 2, 3)))
    graft_ratio = jnp.sqrt(grad_sq) / (jnp.sqrt(pre_sq) + 1e-06)
    update = graft_ratio[None, :, None, None] * precond
    new_momentum = 0.9 * momentum + update
    direction = (update + 0.9 * new_momentum).astype(jnp.bfloat16)
    return (new_momentum, direction)
```

```python
import jax
import jax.numpy as jnp
from jax import lax
from jax.experimental import pallas as pl
from jax.experimental.pallas import tpu as pltpu
from jax.sharding import PartitionSpec as P

Z, Y, X = 8, 4, 4
PAIRS = Z * Y
ROWS = 16
B = 1024
HALF = B // 2
LANES = 128
TOP = 32767.0
MESH = pl.DeviceIdType.MESH
F32 = jnp.float32
BF16 = jnp.bfloat16
OFFSETS = (0, 1, 7, 2, 6, 3, 5, 4)


def offset_at(i):
    step = (i + 1) // 2
    return lax.rem(step + (1 - i % 2) * (8 - 2 * step), 8)


def block_of(owner_ref, pair):
    found = jnp.int32(0)
    for b in range(PAIRS):
        found = jnp.where(owner_ref[0, b] == pair, b, found)
    return found


def exchange_kernel(
    owner_ref, grads_ref, factor_hbm,
    back_ref, head_ref,
    factor, outgoing, gathered, left, right, left_other, product, coded, heads, sums, seen,
    factor_sem, grad_send, grad_recv, sib_send, sib_recv, fac_send, fac_recv,
    back_send, back_recv, sum_send, sum_recv, head_send, head_recv, local_sem, head_local,
):
    me = lax.axis_index("dp")
    x = lax.axis_index("mp")
    z = me // (2 * Y)
    y = (me // 2) % Y
    c = me % 2
    pair = me // 2
    sibling = {"dp": pair * 2 + (1 - c)}

    def chip(i, dy):
        return lax.rem(z + Z - offset_at(i), Z) * Y + lax.rem(y + dy, Y)

    barrier = pltpu.get_barrier_semaphore()

    @pl.loop(1, PAIRS)
    def _(s):
        k = chip(s // Y, s % Y)
        pl.semaphore_signal(barrier, inc=1, device_id={"dp": k * 2 + c}, device_id_type=MESH)

    pl.semaphore_signal(barrier, inc=1, device_id=sibling, device_id_type=MESH)

    @pl.loop(2, 2 * X)
    def _(s):
        target = {"dp": pair * 2 + lax.rem(c + s, 2), "mp": lax.rem(x + s // 2, X)}
        pl.semaphore_signal(barrier, inc=1, device_id=target, device_id_type=MESH)

    factor_in = pltpu.make_async_copy(factor_hbm, factor, factor_sem)
    factor_in.start()

    @pl.loop(0, PAIRS)
    def _(s):
        outgoing[s] = grads_ref[block_of(owner_ref, chip(s // Y, s % Y))]

    pl.semaphore_wait(barrier, (PAIRS - 1) + 1 + (2 * X - 2))

    own_rows = pltpu.make_async_copy(outgoing.at[0], gathered.at[0, y, c], local_sem)
    own_rows.start()

    @pl.loop(1, PAIRS)
    def _(s):
        i = s // Y
        pltpu.make_async_remote_copy(
            src_ref=outgoing.at[s], dst_ref=gathered.at[i, y, c],
            send_sem=grad_send, recv_sem=grad_recv.at[i],
            device_id={"dp": chip(i, s % Y) * 2 + c}, device_id_type=MESH,
        ).start()

    factor_in.wait()

    def split(part_ref, at, value):
        high = value.astype(BF16)
        part_ref[(0,) + at] = high
        part_ref[(1,) + at] = (value - high.astype(F32)).astype(BF16)

    @pl.when(c == 0)
    def _():
        @pl.loop(0, Z)
        def _(i):
            zi = lax.rem(z + offset_at(i), Z)
            for j in range(Z):
                zj = lax.rem(z + OFFSETS[j], Z)
                cols = pl.ds(pl.multiple_of(zj * LANES, LANES), LANES)
                to = pl.ds(j * LANES, LANES)
                split(left, (i, slice(None), slice(None), to), factor[zi, :, 0, :, cols])
                split(left_other, (i, slice(None), slice(None), to), factor[zi, :, 1, :, cols])
            pltpu.make_async_remote_copy(
                src_ref=left_other.at[:, i], dst_ref=left.at[:, i],
                send_sem=fac_send, recv_sem=fac_recv,
                device_id=sibling, device_id_type=MESH,
            ).start()

    @pl.when(c == 1)
    def _():
        @pl.loop(0, Z)
        def _(i):
            for q in range(Y):
                for h in range(2):
                    split(right, (i, q, h), factor[i, q, h])
            pltpu.make_async_remote_copy(
                src_ref=right.at[:, i], dst_ref=right.at[:, i],
                send_sem=fac_send, recv_sem=fac_recv,
                device_id=sibling, device_id_type=MESH,
            ).start()

    def whole(ref, send, recv):
        return pltpu.make_async_remote_copy(
            src_ref=ref, dst_ref=ref, send_sem=send, recv_sem=recv,
            device_id=sibling, device_id_type=MESH,
        )

    own_rows.wait()

    def pass_on(i):
        @pl.when(i == 0)
        def _():
            whole(gathered.at[0, pl.ds(0, Y - 1), 0], grad_send, grad_recv.at[0]).wait_recv()

        @pl.when(i > 0)
        def _():
            whole(gathered.at[i, :, 0], grad_send, grad_recv.at[i]).wait_recv()

        pltpu.make_async_remote_copy(
            src_ref=gathered.at[i, :, c], dst_ref=gathered.at[i, :, c],
            send_sem=sib_send, recv_sem=sib_recv.at[i],
            device_id=sibling, device_id_type=MESH,
        ).start()

    @pl.loop(0, 2)
    def _(i):
        pass_on(i)

    @pl.when(c == 0)
    def _():
        whole(right, fac_send, fac_recv).wait_recv()

    @pl.when(c == 1)
    def _():
        whole(left, fac_send, fac_recv).wait_recv()

    @pl.loop(0, Y)
    def _(j):
        @pl.when(j > 0)
        def _():
            pass_on(2 * j)
            pass_on(2 * j + 1)

        whole(gathered.at[2 * j, :, 0], sib_send, sib_recv.at[2 * j]).wait_recv()
        whole(gathered.at[2 * j + 1, :, 0], sib_send, sib_recv.at[2 * j + 1]).wait_recv()
        some = gathered[pl.ds(2 * j, 2)].reshape(2 * LANES, B)
        cols = pl.ds(pl.multiple_of(j * 2 * LANES, 2 * LANES), 2 * LANES)
        rows = left[:, :, :, :, cols].reshape(B, 2 * LANES)
        term = jnp.dot(rows, some, preferred_element_type=F32)
        term = term[:HALF] + term[HALF:]

        @pl.when(j == 0)
        def _():
            product[...] = term

        @pl.when(j > 0)
        def _():
            product[...] += term

    seen[...] = jnp.zeros_like(seen)
    lane = lax.broadcasted_iota(jnp.int32, (ROWS, LANES), 1)
    diagonal = lane == lax.broadcasted_iota(jnp.int32, (ROWS, LANES), 0)

    @pl.loop(0, Y)
    def _(j):
        base = pl.multiple_of(j * LANES, LANES)
        rows = product[pl.ds(base, LANES)]
        high = rows.astype(BF16)
        low = (rows - high.astype(F32)).astype(BF16)
        both = jnp.concatenate([high, low], axis=0)
        by_high = jnp.dot(both, right[0].reshape(B, B), preferred_element_type=F32)
        by_low = jnp.dot(high, right[1].reshape(B, B), preferred_element_type=F32)
        product[pl.ds(base, LANES)] = by_high[:LANES] + (by_high[LANES:] + by_low)

        @pl.loop(0, 2 * Y)
        def _(q):
            s = j * 2 * Y + q
            value = product[pl.ds(pl.multiple_of(s * ROWS, ROWS), ROWS)]
            seen[...] += _fold(value * value)
            size = jnp.abs(value)
            top = jnp.maximum(jnp.max(size, axis=1, keepdims=True), 1e-37)
            heads[s, 0:1] = jnp.sum(jnp.where(diagonal, jnp.broadcast_to(top, (ROWS, LANES)), 0.0), axis=0, keepdims=True)
            code = (jnp.sqrt(size * (1.0 / top)) * TOP + 0.5).astype(jnp.int32)
            code = jnp.where(value < 0.0, -code, code)
            coded[s] = (code[:, :HALF] & 0xFFFF) | (code[:, HALF:] << 16)
            i = s // Y
            k = lax.rem(z + offset_at(i), Z) * Y + s % Y

            @pl.when(k != pair)
            def _():
                pltpu.make_async_remote_copy(
                    src_ref=coded.at[s], dst_ref=back_ref.at[pair],
                    send_sem=back_send, recv_sem=back_recv,
                    device_id={"dp": k * 2 + c}, device_id_type=MESH,
                ).start()

            @pl.when(k == pair)
            def _():
                pltpu.make_async_copy(coded.at[s], back_ref.at[pair], local_sem).start()

    block = block_of(owner_ref, pair)

    def grad_sum(i, total):
        rows = gathered[i, :, pl.ds(c, 1)].reshape(Y * ROWS, B).astype(F32)
        return total + _fold(rows * rows)

    grad_sq = jnp.sum(lax.fori_loop(0, Z, grad_sum, jnp.zeros((8, LANES), F32)))
    pre_sq = jnp.sum(seen[...])
    one = lax.broadcasted_iota(jnp.int32, (1, LANES), 1)
    sums[0] = jnp.where(one == block, pre_sq, 0.0) + jnp.where(one == block + 64, grad_sq, 0.0)

    @pl.loop(1, 2 * X)
    def _(s):
        target = {"dp": pair * 2 + lax.rem(c + s, 2), "mp": lax.rem(x + s // 2, X)}
        pltpu.make_async_remote_copy(
            src_ref=sums.at[0], dst_ref=sums.at[s],
            send_sem=sum_send, recv_sem=sum_recv,
            device_id=target, device_id_type=MESH,
        ).start()

    whole(sums.at[pl.ds(1, 2 * X - 1)], sum_send, sum_recv).wait()
    total = jnp.sum(sums[...], axis=0)

    @pl.loop(0, PAIRS)
    def _(s):
        heads[s, 1:2] = total
        k = lax.rem(z + offset_at(s // Y), Z) * Y + s % Y

        @pl.when(k != pair)
        def _():
            pltpu.make_async_remote_copy(
                src_ref=heads.at[s], dst_ref=head_ref.at[pair],
                send_sem=head_send, recv_sem=head_recv,
                device_id={"dp": k * 2 + c}, device_id_type=MESH,
            ).start()

        @pl.when(k == pair)
        def _():
            pltpu.make_async_copy(heads.at[s], head_ref.at[pair], head_local).start()

    others = pl.ds(0, PAIRS - 1)
    whole(outgoing.at[others], grad_send, grad_recv.at[0]).wait_send()
    whole(gathered.at[:, :, 0], sib_send, sib_recv.at[0]).wait_send()

    @pl.when(c == 0)
    def _():
        whole(left_other, fac_send, fac_recv).wait_send()

    @pl.when(c == 1)
    def _():
        whole(right, fac_send, fac_recv).wait_send()

    pltpu.make_async_copy(coded.at[0], back_ref.at[pair], local_sem).wait()
    pltpu.make_async_copy(heads.at[0], head_ref.at[pair], head_local).wait()
    whole(back_ref.at[others], back_send, back_recv).wait()
    whole(head_ref.at[others], head_send, head_recv).wait()


def _fold(value):
    total = jnp.zeros((8, LANES), F32)
    for r in range(0, value.shape[0], 8):
        for q in range(0, value.shape[1], LANES):
            total = total + value[r:r + 8, q:q + LANES]
    return total


def exchange(owner, grads, factor):
    grads_words = (PAIRS, ROWS, B)
    return pl.pallas_call(
        exchange_kernel,
        out_shape=(
            jax.ShapeDtypeStruct((PAIRS, ROWS, HALF), jnp.int32),
            jax.ShapeDtypeStruct((PAIRS, 2, LANES), F32),
        ),
        in_specs=[
            pl.BlockSpec(memory_space=pltpu.SMEM),
            pl.BlockSpec(memory_space=pltpu.VMEM),
            pl.BlockSpec(memory_space=pl.ANY),
        ],
        out_specs=[pl.BlockSpec(memory_space=pltpu.VMEM)] * 2,
        scratch_shapes=[
            pltpu.VMEM((Z, Y, 2, ROWS, B), F32),
            pltpu.VMEM(grads_words, BF16),
            pltpu.VMEM((Z, Y, 2, ROWS, B), BF16),
            pltpu.VMEM((2, Z, Y, ROWS, B), BF16),
            pltpu.VMEM((2, Z, Y, 2, ROWS, B), BF16),
            pltpu.VMEM((2, Z, Y, ROWS, B), BF16),
            pltpu.VMEM((HALF, B), F32),
            pltpu.VMEM((PAIRS, ROWS, HALF), jnp.int32),
            pltpu.VMEM((PAIRS, 2, LANES), F32),
            pltpu.VMEM((2 * X, 1, LANES), F32),
            pltpu.VMEM((8, LANES), F32),
            pltpu.SemaphoreType.DMA,
            pltpu.SemaphoreType.DMA,
            pltpu.SemaphoreType.DMA((Z,)),
            pltpu.SemaphoreType.DMA,
            pltpu.SemaphoreType.DMA((Z,)),
            pltpu.SemaphoreType.DMA,
            pltpu.SemaphoreType.DMA,
            pltpu.SemaphoreType.DMA,
            pltpu.SemaphoreType.DMA,
            pltpu.SemaphoreType.DMA,
            pltpu.SemaphoreType.DMA,
            pltpu.SemaphoreType.DMA,
            pltpu.SemaphoreType.DMA,
            pltpu.SemaphoreType.DMA,
            pltpu.SemaphoreType.DMA,
        ],
        compiler_params=pltpu.CompilerParams(
            collective_id=0, has_side_effects=True, vmem_limit_bytes=48 * 1024 * 1024
        ),
        name="exchange",
    )(owner, grads, factor)


STEP = 8


def update_kernel(owner_ref, back_ref, head_ref, momentum_ref, new_ref, direction_ref, graft):
    lane = lax.broadcasted_iota(jnp.int32, (ROWS, LANES), 1)
    diagonal = lane == lax.broadcasted_iota(jnp.int32, (ROWS, LANES), 0)
    one = lax.broadcasted_iota(jnp.int32, (1, LANES), 1)

    @pl.when(pl.program_id(0) == 0)
    def _():
        totals = jnp.sum(head_ref[...], axis=0)[1:2]
        grad = pltpu.roll(totals, 64, 1)
        graft[...] = jnp.sqrt(grad) / (jnp.sqrt(totals) + 1e-06)

    @pl.loop(0, STEP)
    def _(q):
        b = pl.program_id(0) * STEP + q
        k = owner_ref[0, b]
        ratio = jnp.sum(jnp.where(one == b, graft[...], 0.0), axis=1, keepdims=True)
        top = jnp.broadcast_to(head_ref[k][0:1], (ROWS, LANES))
        top = jnp.sum(jnp.where(diagonal, top, 0.0), axis=1, keepdims=True)
        scale = top * (ratio * (1.0 / (TOP * TOP)))
        words = back_ref[k]
        for h, code in enumerate(((words << 16) >> 16, words >> 16)):
            at = pl.ds(h * HALF, HALF)
            code = code.astype(F32)
            update = code * jnp.abs(code) * scale
            new = 0.9 * momentum_ref[q, :, at] + update
            new_ref[q, :, at] = new
            direction_ref[q, :, at] = (update + 0.9 * new).astype(BF16)


def apply_update(owner, back, head, momentum):
    block = pl.BlockSpec((STEP, ROWS, B), lambda i: (i, 0, 0))
    return pl.pallas_call(
        update_kernel,
        grid=(PAIRS // STEP,),
        out_shape=(
            jax.ShapeDtypeStruct((PAIRS, ROWS, B), F32),
            jax.ShapeDtypeStruct((PAIRS, ROWS, B), BF16),
        ),
        in_specs=[
            pl.BlockSpec(memory_space=pltpu.SMEM),
            pl.BlockSpec(memory_space=pltpu.VMEM),
            pl.BlockSpec(memory_space=pltpu.VMEM),
            block,
        ],
        out_specs=[block, block],
        scratch_shapes=[pltpu.VMEM((1, LANES), F32)],
        compiler_params=pltpu.CompilerParams(vmem_limit_bytes=24 * 1024 * 1024),
        name="update",
    )(owner, back, head, momentum)


def per_device(grads, momentum, root_factors, owner_table):
    factor = root_factors.reshape(Z, Y, 2, ROWS, B)
    back, head = exchange(owner_table, grads[0], factor)
    new_momentum, direction = apply_update(owner_table, back, head, momentum[0])
    return (new_momentum[None], direction[None])


def solution(mesh):
    in_specs = (
        P("mp", None, "dp", None),
        P("mp", None, "dp", None),
        P("mp", "dp", None, None),
        P("mp", None),
    )
    out_specs = (P("mp", None, "dp", None), P("mp", None, "dp", None))
    return jax.shard_map(
        per_device, mesh=mesh, in_specs=in_specs, out_specs=out_specs, check_vma=False
    )
```

```python
import jax
import jax.numpy as jnp
from jax import lax
from jax.experimental import pallas as pl
from jax.experimental.pallas import tpu as pltpu
from jax.sharding import PartitionSpec as P

Z, Y, X = 8, 4, 4
PAIRS = Z * Y
ROWS = 16
B = 1024
HALF = B // 2
LANES = 128
TOP = 32767.0
MESH = pl.DeviceIdType.MESH
F32 = jnp.float32
BF16 = jnp.bfloat16
OFFSETS = (3, 5, 4, 0, 2, 6, 1, 7)
OWN = OFFSETS.index(0)
PACKED = 6


def offset_at(i):
    found = jnp.int32(OFFSETS[0])
    for n in range(1, Z):
        found = jnp.where(i == n, OFFSETS[n], found)
    return found


def packed_inverse(owner_row):
    lane = lax.broadcasted_iota(jnp.int32, (1, PAIRS), 1)
    words = []
    for w in range((PAIRS + PACKED - 1) // PACKED):
        at = owner_row - PACKED * w
        inside = (at >= 0) & (at < PACKED)
        shift = 5 * jnp.where(inside, at, 0)
        words.append(jnp.sum(jnp.where(inside, lane << shift, 0)))
    return words


def exchange_kernel(
    owner_hbm, grads_hbm, factor_hbm,
    back_ref, head_ref,
    owner_rows, grads_ref, inverse, factor, outgoing, gathered, left, right, left_other, product, coded, heads, sums, seen,
    owner_sem, grads_sem, factor_sem, grad_send, grad_recv, sib_send, sib_recv, fac_send, fac_recv,
    back_send, back_recv, sum_send, sum_recv, head_send, head_recv, local_sem, head_local,
):
    me = lax.axis_index("dp")
    x = lax.axis_index("mp")
    z = me // (2 * Y)
    y = (me // 2) % Y
    c = me % 2
    pair = me // 2
    sibling = {"dp": pair * 2 + (1 - c)}

    def chip(i, dy):
        return lax.rem(z + Z - OFFSETS[i], Z) * Y + lax.rem(y + dy, Y)

    owner_in = pltpu.make_async_copy(owner_hbm, owner_rows, owner_sem)
    owner_in.start()
    grads_in = pltpu.make_async_copy(grads_hbm, grads_ref, grads_sem)
    grads_in.start()

    barrier = pltpu.get_barrier_semaphore()

    partners = [(i, dy) for i in range(Z) for dy in range(Y) if (OFFSETS[i], dy) != (0, 0)]
    for i, dy in partners:
        pl.semaphore_signal(barrier, inc=1, device_id={"dp": chip(i, dy) * 2 + c}, device_id_type=MESH)

    pl.semaphore_signal(barrier, inc=1, device_id=sibling, device_id_type=MESH)

    @pl.loop(2, 2 * X)
    def _(s):
        target = {"dp": pair * 2 + lax.rem(c + s, 2), "mp": lax.rem(x + s // 2, X)}
        pl.semaphore_signal(barrier, inc=1, device_id=target, device_id_type=MESH)

    factor_in = pltpu.make_async_copy(factor_hbm, factor, factor_sem)
    factor_in.start()

    owner_in.wait()
    words = packed_inverse(owner_rows[...])
    for w, word in enumerate(words):
        inverse[w] = word
    grads_in.wait()
    for k in range(PAIRS):
        outgoing[k] = grads_ref[(words[k // PACKED] >> (5 * (k % PACKED))) & (PAIRS - 1)]

    pl.semaphore_wait(barrier, (PAIRS - 1) + 1 + (2 * X - 2))

    for i, dy in partners:
        k = chip(i, dy)
        pltpu.make_async_remote_copy(
            src_ref=outgoing.at[k], dst_ref=gathered.at[i, y, c],
            send_sem=grad_send, recv_sem=grad_recv.at[i],
            device_id={"dp": k * 2 + c}, device_id_type=MESH,
        ).start()
    own_rows = pltpu.make_async_copy(outgoing.at[pair], gathered.at[OWN, y, c], local_sem)
    own_rows.start()

    factor_in.wait()

    def split(part_ref, at, value):
        high = value.astype(BF16)
        part_ref[(0,) + at] = high
        part_ref[(1,) + at] = (value - high.astype(F32)).astype(BF16)

    @pl.when(c == 0)
    def _():
        @pl.loop(0, Z)
        def _(i):
            zi = lax.rem(z + offset_at(i), Z)
            for j in range(Z):
                zj = lax.rem(z + OFFSETS[j], Z)
                cols = pl.ds(pl.multiple_of(zj * LANES, LANES), LANES)
                to = pl.ds(j * LANES, LANES)
                split(left, (i, slice(None), slice(None), to), factor[zi, :, 0, :, cols])
                split(left_other, (i, slice(None), slice(None), to), factor[zi, :, 1, :, cols])
            pltpu.make_async_remote_copy(
                src_ref=left_other.at[:, i], dst_ref=left.at[:, i],
                send_sem=fac_send, recv_sem=fac_recv,
                device_id=sibling, device_id_type=MESH,
            ).start()

    @pl.when(c == 1)
    def _():
        @pl.loop(0, Z)
        def _(i):
            for q in range(Y):
                for h in range(2):
                    split(right, (i, q, h), factor[i, q, h])
            pltpu.make_async_remote_copy(
                src_ref=right.at[:, i], dst_ref=right.at[:, i],
                send_sem=fac_send, recv_sem=fac_recv,
                device_id=sibling, device_id_type=MESH,
            ).start()

    def whole(ref, send, recv):
        return pltpu.make_async_remote_copy(
            src_ref=ref, dst_ref=ref, send_sem=send, recv_sem=recv,
            device_id=sibling, device_id_type=MESH,
        )

    own_rows.wait()

    def pass_on(i):
        if i == OWN:
            whole(gathered.at[i, pl.ds(0, Y - 1), 0], grad_send, grad_recv.at[i]).wait_recv()
        else:
            whole(gathered.at[i, :, 0], grad_send, grad_recv.at[i]).wait_recv()
        pltpu.make_async_remote_copy(
            src_ref=gathered.at[i, :, c], dst_ref=gathered.at[i, :, c],
            send_sem=sib_send, recv_sem=sib_recv.at[i],
            device_id=sibling, device_id_type=MESH,
        ).start()

    pass_on(0)
    pass_on(1)

    @pl.when(c == 0)
    def _():
        whole(right, fac_send, fac_recv).wait_recv()

    @pl.when(c == 1)
    def _():
        whole(left, fac_send, fac_recv).wait_recv()

    for j in range(Y):
        if j > 0:
            pass_on(2 * j)
            pass_on(2 * j + 1)
        whole(gathered.at[2 * j, :, 0], sib_send, sib_recv.at[2 * j]).wait_recv()
        whole(gathered.at[2 * j + 1, :, 0], sib_send, sib_recv.at[2 * j + 1]).wait_recv()
        some = gathered[2 * j:2 * j + 2].reshape(2 * LANES, B)
        rows = left[:, :, :, :, j * 2 * LANES:(j + 1) * 2 * LANES].reshape(B, 2 * LANES)
        term = jnp.dot(rows, some, preferred_element_type=F32)
        term = term[:HALF] + term[HALF:]
        if j == 0:
            product[...] = term
        else:
            product[...] += term

    seen[...] = jnp.zeros_like(seen)
    lane = lax.broadcasted_iota(jnp.int32, (ROWS, LANES), 1)
    diagonal = lane == lax.broadcasted_iota(jnp.int32, (ROWS, LANES), 0)

    @pl.loop(0, Y)
    def _(j):
        base = pl.multiple_of(j * LANES, LANES)
        rows = product[pl.ds(base, LANES)]
        high = rows.astype(BF16)
        low = (rows - high.astype(F32)).astype(BF16)
        both = jnp.concatenate([high, low], axis=0)
        by_high = jnp.dot(both, right[0].reshape(B, B), preferred_element_type=F32)
        by_low = jnp.dot(high, right[1].reshape(B, B), preferred_element_type=F32)
        product[pl.ds(base, LANES)] = by_high[:LANES] + (by_high[LANES:] + by_low)

        @pl.loop(0, 2 * Y)
        def _(q):
            s = j * 2 * Y + q
            value = product[pl.ds(pl.multiple_of(s * ROWS, ROWS), ROWS)]
            seen[...] += _fold(value * value)
            size = jnp.abs(value)
            top = jnp.maximum(jnp.max(size, axis=1, keepdims=True), 1e-37)
            heads[s, 0:1] = jnp.sum(jnp.where(diagonal, jnp.broadcast_to(top, (ROWS, LANES)), 0.0), axis=0, keepdims=True)
            code = (jnp.sqrt(size * (1.0 / top)) * TOP + 0.5).astype(jnp.int32)
            code = jnp.where(value < 0.0, -code, code)
            coded[s] = (code[:, :HALF] & 0xFFFF) | (code[:, HALF:] << 16)
            i = s // Y
            k = lax.rem(z + offset_at(i), Z) * Y + s % Y

            @pl.when(k != pair)
            def _():
                pltpu.make_async_remote_copy(
                    src_ref=coded.at[s], dst_ref=back_ref.at[pair],
                    send_sem=back_send, recv_sem=back_recv,
                    device_id={"dp": k * 2 + c}, device_id_type=MESH,
                ).start()

            @pl.when(k == pair)
            def _():
                pltpu.make_async_copy(coded.at[s], back_ref.at[pair], local_sem).start()

    block = (inverse[pair // PACKED] >> (5 * (pair % PACKED))) & (PAIRS - 1)

    def grad_sum(i, total):
        rows = gathered[i, :, pl.ds(c, 1)].reshape(Y * ROWS, B).astype(F32)
        return total + _fold(rows * rows)

    grad_sq = jnp.sum(lax.fori_loop(0, Z, grad_sum, jnp.zeros((8, LANES), F32)))
    pre_sq = jnp.sum(seen[...])
    one = lax.broadcasted_iota(jnp.int32, (1, LANES), 1)
    sums[0] = jnp.where(one == block, pre_sq, 0.0) + jnp.where(one == block + 64, grad_sq, 0.0)

    @pl.loop(1, 2 * X)
    def _(s):
        target = {"dp": pair * 2 + lax.rem(c + s, 2), "mp": lax.rem(x + s // 2, X)}
        pltpu.make_async_remote_copy(
            src_ref=sums.at[0], dst_ref=sums.at[s],
            send_sem=sum_send, recv_sem=sum_recv,
            device_id=target, device_id_type=MESH,
        ).start()

    whole(sums.at[pl.ds(1, 2 * X - 1)], sum_send, sum_recv).wait()
    total = jnp.sum(sums[...], axis=0)

    @pl.loop(0, PAIRS)
    def _(s):
        heads[s, 1:2] = total
        k = lax.rem(z + offset_at(s // Y), Z) * Y + s % Y

        @pl.when(k != pair)
        def _():
            pltpu.make_async_remote_copy(
                src_ref=heads.at[s], dst_ref=head_ref.at[pair],
                send_sem=head_send, recv_sem=head_recv,
                device_id={"dp": k * 2 + c}, device_id_type=MESH,
            ).start()

        @pl.when(k == pair)
        def _():
            pltpu.make_async_copy(heads.at[s], head_ref.at[pair], head_local).start()

    others = pl.ds(0, PAIRS - 1)
    whole(outgoing.at[others], grad_send, grad_recv.at[0]).wait_send()
    whole(gathered.at[:, :, 0], sib_send, sib_recv.at[0]).wait_send()

    @pl.when(c == 0)
    def _():
        whole(left_other, fac_send, fac_recv).wait_send()

    @pl.when(c == 1)
    def _():
        whole(right, fac_send, fac_recv).wait_send()

    pltpu.make_async_copy(coded.at[0], back_ref.at[pair], local_sem).wait()
    pltpu.make_async_copy(heads.at[0], head_ref.at[pair], head_local).wait()
    whole(back_ref.at[others], back_send, back_recv).wait()
    whole(head_ref.at[others], head_send, head_recv).wait()


def _fold(value):
    total = jnp.zeros((8, LANES), F32)
    for r in range(0, value.shape[0], 8):
        for q in range(0, value.shape[1], LANES):
            total = total + value[r:r + 8, q:q + LANES]
    return total


def exchange(owner, grads, factor):
    grads_words = (PAIRS, ROWS, B)
    return pl.pallas_call(
        exchange_kernel,
        out_shape=(
            jax.ShapeDtypeStruct((PAIRS, ROWS, HALF), jnp.int32),
            jax.ShapeDtypeStruct((PAIRS, 2, LANES), F32),
        ),
        in_specs=[
            pl.BlockSpec(memory_space=pltpu.HBM),
            pl.BlockSpec(memory_space=pltpu.HBM),
            pl.BlockSpec(memory_space=pltpu.HBM),
        ],
        out_specs=[pl.BlockSpec(memory_space=pltpu.VMEM)] * 2,
        scratch_shapes=[
            pltpu.VMEM((1, PAIRS), jnp.int32),
            pltpu.VMEM(grads_words, BF16),
            pltpu.SMEM((PACKED,), jnp.int32),
            pltpu.VMEM((Z, Y, 2, ROWS, B), F32),
            pltpu.VMEM(grads_words, BF16),
            pltpu.VMEM((Z, Y, 2, ROWS, B), BF16),
            pltpu.VMEM((2, Z, Y, ROWS, B), BF16),
            pltpu.VMEM((2, Z, Y, 2, ROWS, B), BF16),
            pltpu.VMEM((2, Z, Y, ROWS, B), BF16),
            pltpu.VMEM((HALF, B), F32),
            pltpu.VMEM((PAIRS, ROWS, HALF), jnp.int32),
            pltpu.VMEM((PAIRS, 2, LANES), F32),
            pltpu.VMEM((2 * X, 1, LANES), F32),
            pltpu.VMEM((8, LANES), F32),
            pltpu.SemaphoreType.DMA,
            pltpu.SemaphoreType.DMA,
            pltpu.SemaphoreType.DMA,
            pltpu.SemaphoreType.DMA,
            pltpu.SemaphoreType.DMA((Z,)),
            pltpu.SemaphoreType.DMA,
            pltpu.SemaphoreType.DMA((Z,)),
            pltpu.SemaphoreType.DMA,
            pltpu.SemaphoreType.DMA,
            pltpu.SemaphoreType.DMA,
            pltpu.SemaphoreType.DMA,
            pltpu.SemaphoreType.DMA,
            pltpu.SemaphoreType.DMA,
            pltpu.SemaphoreType.DMA,
            pltpu.SemaphoreType.DMA,
            pltpu.SemaphoreType.DMA,
            pltpu.SemaphoreType.DMA,
        ],
        compiler_params=pltpu.CompilerParams(
            collective_id=0, has_side_effects=True, vmem_limit_bytes=48 * 1024 * 1024
        ),
        name="exchange",
    )(owner, grads, factor)


STEP = 4


def update_kernel(owner_ref, back_ref, head_ref, momentum_ref, new_hbm, direction_hbm, new, direction, scales, sem):
    lane = lax.broadcasted_iota(jnp.int32, (ROWS, LANES), 1)
    diagonal = lane == lax.broadcasted_iota(jnp.int32, (ROWS, LANES), 0)
    heads = head_ref[...]
    totals = jnp.sum(heads, axis=0)[1:2]
    grad = pltpu.roll(totals, 64, 1)
    graft = jnp.sqrt(grad) / (jnp.sqrt(totals) + 1e-06) * (1.0 / (TOP * TOP))
    for k in range(PAIRS):
        top = jnp.broadcast_to(heads[k, 0:1], (ROWS, LANES))
        top = jnp.sum(jnp.where(diagonal, top, 0.0), axis=1, keepdims=True)
        scales[k] = jnp.broadcast_to(top, (ROWS, LANES))
    copies = []
    for b in range(PAIRS):
        k = owner_ref[0, b]
        scale = scales[k] * jnp.broadcast_to(graft[:, b:b + 1], (ROWS, LANES))
        words = back_ref[k]
        for h, code in enumerate(((words << 16) >> 16, words >> 16)):
            code = code.astype(F32)
            code = code * jnp.abs(code)
            for q in range(HALF // LANES):
                at = slice(h * HALF + q * LANES, h * HALF + (q + 1) * LANES)
                update = code[:, q * LANES:(q + 1) * LANES] * scale
                fresh = 0.9 * momentum_ref[b, :, at] + update
                new[b, :, at] = fresh
                direction[b, :, at] = (update + 0.9 * fresh).astype(BF16)
        if (b + 1) % STEP == 0:
            part = pl.ds(b + 1 - STEP, STEP)
            for n, (have, give) in enumerate(((new, new_hbm), (direction, direction_hbm))):
                copies.append(pltpu.make_async_copy(have.at[part], give.at[part], sem.at[n, b // STEP]))
                copies[-1].start()
    for copy in copies:
        copy.wait()


def apply_update(owner, back, head, momentum):
    return pl.pallas_call(
        update_kernel,
        out_shape=(
            jax.ShapeDtypeStruct((PAIRS, ROWS, B), F32),
            jax.ShapeDtypeStruct((PAIRS, ROWS, B), BF16),
        ),
        in_specs=[
            pl.BlockSpec(memory_space=pltpu.SMEM),
            pl.BlockSpec(memory_space=pltpu.VMEM),
            pl.BlockSpec(memory_space=pltpu.VMEM),
            pl.BlockSpec(memory_space=pltpu.VMEM),
        ],
        out_specs=[pl.BlockSpec(memory_space=pltpu.HBM)] * 2,
        scratch_shapes=[
            pltpu.VMEM((PAIRS, ROWS, B), F32),
            pltpu.VMEM((PAIRS, ROWS, B), BF16),
            pltpu.VMEM((PAIRS, ROWS, LANES), F32),
            pltpu.SemaphoreType.DMA((2, PAIRS // STEP)),
        ],
        compiler_params=pltpu.CompilerParams(vmem_limit_bytes=24 * 1024 * 1024),
        name="update",
    )(owner, back, head, momentum)


def per_device(grads, momentum, root_factors, owner_table):
    factor = root_factors.reshape(Z, Y, 2, ROWS, B)
    back, head = exchange(owner_table, grads[0], factor)
    new_momentum, direction = apply_update(owner_table, back, head, momentum[0])
    return (new_momentum[None], direction[None])


def solution(mesh):
    in_specs = (
        P("mp", None, "dp", None),
        P("mp", None, "dp", None),
        P("mp", "dp", None, None),
        P("mp", None),
    )
    out_specs = (P("mp", None, "dp", None), P("mp", None, "dp", None))
    return jax.shard_map(
        per_device, mesh=mesh, in_specs=in_specs, out_specs=out_specs, check_vma=False
    )
```

```python
import jax
import jax.numpy as jnp
from jax import lax
from jax.experimental import pallas as pl
from jax.experimental.pallas import tpu as pltpu
from jax.sharding import PartitionSpec as P

Z, Y, X = 8, 4, 4
PAIRS = Z * Y
ROWS = 16
B = 1024
HALF = B // 2
LANES = 128
TOP = 32767.0
MESH = pl.DeviceIdType.MESH
F32 = jnp.float32
BF16 = jnp.bfloat16
OFFSETS = (3, 5, 4, 0, 2, 6, 1, 7)
OWN = OFFSETS.index(0)
PACKED = 6
HELD = PAIRS - 2 * Y


def offset_at(i):
    found = jnp.int32(OFFSETS[0])
    for n in range(1, Z):
        found = jnp.where(i == n, OFFSETS[n], found)
    return found


def packed_inverse(owner_row):
    lane = lax.broadcasted_iota(jnp.int32, (1, PAIRS), 1)
    words = []
    for w in range((PAIRS + PACKED - 1) // PACKED):
        at = owner_row - PACKED * w
        inside = (at >= 0) & (at < PACKED)
        shift = 5 * jnp.where(inside, at, 0)
        words.append(jnp.sum(jnp.where(inside, lane << shift, 0)))
    return words


def exchange_kernel(
    owner_rows, grads_hbm, factor_hbm,
    back_ref, head_ref,
    grads_ref, inverse, factor, outgoing, gathered, left, right, left_other, product, coded, heads, sums, seen,
    grads_sem, factor_sem, grad_send, grad_recv, sib_send, sib_recv, fac_send, fac_recv,
    back_send, back_recv, sum_send, sum_recv, head_send, head_recv, local_sem, head_local,
):
    me = lax.axis_index("dp")
    x = lax.axis_index("mp")
    z = me // (2 * Y)
    y = (me // 2) % Y
    c = me % 2
    pair = me // 2
    sibling = {"dp": pair * 2 + (1 - c)}

    def chip(i, dy):
        return lax.rem(z + Z - OFFSETS[i], Z) * Y + lax.rem(y + dy, Y)

    grads_in = pltpu.make_async_copy(grads_hbm, grads_ref, grads_sem)
    grads_in.start()

    barrier = pltpu.get_barrier_semaphore()

    partners = [(i, dy) for i in range(Z) for dy in range(Y) if (OFFSETS[i], dy) != (0, 0)]
    for i, dy in partners:
        pl.semaphore_signal(barrier, inc=1, device_id={"dp": chip(i, dy) * 2 + c}, device_id_type=MESH)

    pl.semaphore_signal(barrier, inc=1, device_id=sibling, device_id_type=MESH)

    @pl.loop(2, 2 * X)
    def _(s):
        target = {"dp": pair * 2 + lax.rem(c + s, 2), "mp": lax.rem(x + s // 2, X)}
        pl.semaphore_signal(barrier, inc=1, device_id=target, device_id_type=MESH)

    factor_in = pltpu.make_async_copy(factor_hbm, factor, factor_sem)
    factor_in.start()

    words = packed_inverse(owner_rows[...])
    for w, word in enumerate(words):
        inverse[w] = word
    grads_in.wait()
    for k in range(PAIRS):
        outgoing[k] = grads_ref[(words[k // PACKED] >> (5 * (k % PACKED))) & (PAIRS - 1)]

    pl.semaphore_wait(barrier, (PAIRS - 1) + 1 + (2 * X - 2))

    for i, dy in partners:
        k = chip(i, dy)
        pltpu.make_async_remote_copy(
            src_ref=outgoing.at[k], dst_ref=gathered.at[i, y, c],
            send_sem=grad_send, recv_sem=grad_recv.at[i, y],
            device_id={"dp": k * 2 + c}, device_id_type=MESH,
        ).start()
    own_rows = pltpu.make_async_copy(outgoing.at[pair], gathered.at[OWN, y, c], local_sem)
    own_rows.start()

    factor_in.wait()

    def split(part_ref, at, value):
        high = value.astype(BF16)
        part_ref[(0,) + at] = high
        part_ref[(1,) + at] = (value - high.astype(F32)).astype(BF16)

    @pl.when(c == 0)
    def _():
        @pl.loop(0, Z)
        def _(i):
            zi = lax.rem(z + offset_at(i), Z)
            for j in range(Z):
                zj = lax.rem(z + OFFSETS[j], Z)
                cols = pl.ds(pl.multiple_of(zj * LANES, LANES), LANES)
                to = pl.ds(j * LANES, LANES)
                split(left, (i, slice(None), slice(None), to), factor[zi, :, 0, :, cols])
                split(left_other, (i, slice(None), slice(None), to), factor[zi, :, 1, :, cols])
            pltpu.make_async_remote_copy(
                src_ref=left_other.at[:, i], dst_ref=left.at[:, i],
                send_sem=fac_send, recv_sem=fac_recv,
                device_id=sibling, device_id_type=MESH,
            ).start()

    @pl.when(c == 1)
    def _():
        @pl.loop(0, Z)
        def _(i):
            for q in range(Y):
                for h in range(2):
                    split(right, (i, q, h), factor[i, q, h])
            pltpu.make_async_remote_copy(
                src_ref=right.at[:, i], dst_ref=right.at[:, i],
                send_sem=fac_send, recv_sem=fac_recv,
                device_id=sibling, device_id_type=MESH,
            ).start()

    def whole(ref, send, recv):
        return pltpu.make_async_remote_copy(
            src_ref=ref, dst_ref=ref, send_sem=send, recv_sem=recv,
            device_id=sibling, device_id_type=MESH,
        )

    own_rows.wait()

    def arrived(i, dy):
        if (OFFSETS[i], dy) != (0, 0):
            q = lax.rem(y + dy, Y)
            whole(gathered.at[i, q, 0], grad_send, grad_recv.at[i, q]).wait_recv()

    def pass_on(part, i):
        pltpu.make_async_remote_copy(
            src_ref=part, dst_ref=part, send_sem=sib_send, recv_sem=sib_recv.at[i],
            device_id=sibling, device_id_type=MESH,
        ).start()

    def pass_on_two(j):
        if j < Y - 1:
            for i in (2 * j, 2 * j + 1):
                for dy in range(Y):
                    arrived(i, dy)
                pass_on(gathered.at[i, :, c], i)
        else:
            for dy in (0, 1, 3, 2):
                for i in (2 * j, 2 * j + 1):
                    arrived(i, dy)
                    pass_on(gathered.at[i, lax.rem(y + dy, Y), c], i)

    pass_on_two(0)

    @pl.when(c == 0)
    def _():
        whole(right, fac_send, fac_recv).wait_recv()

    @pl.when(c == 1)
    def _():
        whole(left, fac_send, fac_recv).wait_recv()

    for j in range(Y):
        if j > 0:
            pass_on_two(j)
        whole(gathered.at[2 * j, :, 0], sib_send, sib_recv.at[2 * j]).wait_recv()
        whole(gathered.at[2 * j + 1, :, 0], sib_send, sib_recv.at[2 * j + 1]).wait_recv()
        some = gathered[2 * j:2 * j + 2].reshape(2 * LANES, B)
        rows = left[:, :, :, :, j * 2 * LANES:(j + 1) * 2 * LANES].reshape(B, 2 * LANES)
        term = jnp.dot(rows, some, preferred_element_type=F32)
        term = term[:HALF] + term[HALF:]
        if j == 0:
            product[...] = term
        else:
            product[...] += term

    seen[...] = jnp.zeros_like(seen)
    lane = lax.broadcasted_iota(jnp.int32, (ROWS, LANES), 1)
    diagonal = lane == lax.broadcasted_iota(jnp.int32, (ROWS, LANES), 0)

    def partner(s):
        return lax.rem(z + offset_at(s // Y), Z) * Y + s % Y

    def give_back(s):
        k = partner(s)

        @pl.when(k != pair)
        def _():
            pltpu.make_async_remote_copy(
                src_ref=coded.at[s], dst_ref=back_ref.at[pair],
                send_sem=back_send, recv_sem=back_recv,
                device_id={"dp": k * 2 + c}, device_id_type=MESH,
            ).start()

        @pl.when(k == pair)
        def _():
            pltpu.make_async_copy(coded.at[s], back_ref.at[pair], local_sem).start()

    @pl.loop(0, Y)
    def _(j):
        base = pl.multiple_of(j * LANES, LANES)
        rows = product[pl.ds(base, LANES)]
        high = rows.astype(BF16)
        low = (rows - high.astype(F32)).astype(BF16)
        both = jnp.concatenate([high, low], axis=0)
        by_high = jnp.dot(both, right[0].reshape(B, B), preferred_element_type=F32)
        by_low = jnp.dot(high, right[1].reshape(B, B), preferred_element_type=F32)
        product[pl.ds(base, LANES)] = by_high[:LANES] + (by_high[LANES:] + by_low)

        @pl.loop(0, 2 * Y)
        def _(q):
            s = j * 2 * Y + q
            value = product[pl.ds(pl.multiple_of(s * ROWS, ROWS), ROWS)]
            seen[...] += _fold(value * value)
            size = jnp.abs(value)
            top = jnp.maximum(jnp.max(size, axis=1, keepdims=True), 1e-37)
            heads[s, 0:1] = jnp.sum(jnp.where(diagonal, jnp.broadcast_to(top, (ROWS, LANES)), 0.0), axis=0, keepdims=True)
            code = (jnp.sqrt(size * (1.0 / top)) * TOP + 0.5).astype(jnp.int32)
            code = jnp.where(value < 0.0, -code, code)
            coded[s] = (code[:, :HALF] & 0xFFFF) | (code[:, HALF:] << 16)

            @pl.when(s < HELD)
            def _():
                give_back(s)

    block = (inverse[pair // PACKED] >> (5 * (pair % PACKED))) & (PAIRS - 1)

    def grad_sum(i, total):
        rows = gathered[i, :, pl.ds(c, 1)].reshape(Y * ROWS, B).astype(F32)
        return total + _fold(rows * rows)

    grad_sq = jnp.sum(lax.fori_loop(0, Z, grad_sum, jnp.zeros((8, LANES), F32)))
    pre_sq = jnp.sum(seen[...])
    one = lax.broadcasted_iota(jnp.int32, (1, LANES), 1)
    sums[0] = jnp.where(one == block, pre_sq, 0.0) + jnp.where(one == block + 64, grad_sq, 0.0)

    @pl.loop(1, 2 * X)
    def _(s):
        target = {"dp": pair * 2 + lax.rem(c + s, 2), "mp": lax.rem(x + s // 2, X)}
        pltpu.make_async_remote_copy(
            src_ref=sums.at[0], dst_ref=sums.at[s],
            send_sem=sum_send, recv_sem=sum_recv,
            device_id=target, device_id_type=MESH,
        ).start()

    whole(sums.at[pl.ds(1, 2 * X - 1)], sum_send, sum_recv).wait()
    total = jnp.sum(sums[...], axis=0)

    @pl.loop(0, PAIRS)
    def _(s):
        heads[s, 1:2] = total
        k = partner(s)

        @pl.when(k != pair)
        def _():
            pltpu.make_async_remote_copy(
                src_ref=heads.at[s], dst_ref=head_ref.at[pair],
                send_sem=head_send, recv_sem=head_recv,
                device_id={"dp": k * 2 + c}, device_id_type=MESH,
            ).start()

        @pl.when(k == pair)
        def _():
            pltpu.make_async_copy(heads.at[s], head_ref.at[pair], head_local).start()

    @pl.loop(HELD, PAIRS)
    def _(s):
        give_back(s)

    others = pl.ds(0, PAIRS - 1)
    whole(outgoing.at[others], grad_send, grad_recv.at[0, 0]).wait_send()
    whole(gathered.at[:, :, 0], sib_send, sib_recv.at[0]).wait_send()

    @pl.when(c == 0)
    def _():
        whole(left_other, fac_send, fac_recv).wait_send()

    @pl.when(c == 1)
    def _():
        whole(right, fac_send, fac_recv).wait_send()

    pltpu.make_async_copy(coded.at[0], back_ref.at[pair], local_sem).wait()
    pltpu.make_async_copy(heads.at[0], head_ref.at[pair], head_local).wait()
    whole(back_ref.at[others], back_send, back_recv).wait()
    whole(head_ref.at[others], head_send, head_recv).wait()


def _fold(value):
    total = jnp.zeros((8, LANES), F32)
    for r in range(0, value.shape[0], 8):
        for q in range(0, value.shape[1], LANES):
            total = total + value[r:r + 8, q:q + LANES]
    return total


def exchange(owner, grads, factor):
    grads_words = (PAIRS, ROWS, B)
    return pl.pallas_call(
        exchange_kernel,
        out_shape=(
            jax.ShapeDtypeStruct((PAIRS, ROWS, HALF), jnp.int32),
            jax.ShapeDtypeStruct((PAIRS, 2, LANES), F32),
        ),
        in_specs=[
            pl.BlockSpec(memory_space=pltpu.VMEM),
            pl.BlockSpec(memory_space=pltpu.HBM),
            pl.BlockSpec(memory_space=pltpu.HBM),
        ],
        out_specs=[pl.BlockSpec(memory_space=pltpu.VMEM)] * 2,
        scratch_shapes=[
            pltpu.VMEM(grads_words, BF16),
            pltpu.SMEM((PACKED,), jnp.int32),
            pltpu.VMEM((Z, Y, 2, ROWS, B), F32),
            pltpu.VMEM(grads_words, BF16),
            pltpu.VMEM((Z, Y, 2, ROWS, B), BF16),
            pltpu.VMEM((2, Z, Y, ROWS, B), BF16),
            pltpu.VMEM((2, Z, Y, 2, ROWS, B), BF16),
            pltpu.VMEM((2, Z, Y, ROWS, B), BF16),
            pltpu.VMEM((HALF, B), F32),
            pltpu.VMEM((PAIRS, ROWS, HALF), jnp.int32),
            pltpu.VMEM((PAIRS, 2, LANES), F32),
            pltpu.VMEM((2 * X, 1, LANES), F32),
            pltpu.VMEM((8, LANES), F32),
            pltpu.SemaphoreType.DMA,
            pltpu.SemaphoreType.DMA,
            pltpu.SemaphoreType.DMA,
            pltpu.SemaphoreType.DMA((Z, Y)),
            pltpu.SemaphoreType.DMA,
            pltpu.SemaphoreType.DMA((Z,)),
            pltpu.SemaphoreType.DMA,
            pltpu.SemaphoreType.DMA,
            pltpu.SemaphoreType.DMA,
            pltpu.SemaphoreType.DMA,
            pltpu.SemaphoreType.DMA,
            pltpu.SemaphoreType.DMA,
            pltpu.SemaphoreType.DMA,
            pltpu.SemaphoreType.DMA,
            pltpu.SemaphoreType.DMA,
            pltpu.SemaphoreType.DMA,
        ],
        compiler_params=pltpu.CompilerParams(
            collective_id=0, has_side_effects=True, vmem_limit_bytes=52 * 1024 * 1024
        ),
        name="exchange",
    )(owner, grads, factor)


STEP = 4


def update_kernel(owner_in, back_ref, head_ref, momentum_ref, new_hbm, direction_hbm, owner_ref, new, direction, scales, owner_sem, sem):
    owner = pltpu.make_async_copy(owner_in, owner_ref, owner_sem)
    owner.start()
    lane = lax.broadcasted_iota(jnp.int32, (ROWS, LANES), 1)
    diagonal = lane == lax.broadcasted_iota(jnp.int32, (ROWS, LANES), 0)
    heads = head_ref[...]
    totals = jnp.sum(heads, axis=0)[1:2]
    grad = pltpu.roll(totals, 64, 1)
    graft = jnp.sqrt(grad) / (jnp.sqrt(totals) + 1e-06) * (1.0 / (TOP * TOP))
    for k in range(PAIRS):
        top = jnp.broadcast_to(heads[k, 0:1], (ROWS, LANES))
        top = jnp.sum(jnp.where(diagonal, top, 0.0), axis=1, keepdims=True)
        scales[k] = jnp.broadcast_to(top, (ROWS, LANES))
    owner.wait()
    copies = []
    for b in range(PAIRS):
        k = owner_ref[0, b]
        scale = scales[k] * jnp.broadcast_to(graft[:, b:b + 1], (ROWS, LANES))
        words = back_ref[k]
        for h, code in enumerate(((words << 16) >> 16, words >> 16)):
            code = code.astype(F32)
            code = code * jnp.abs(code)
            for q in range(HALF // LANES):
                at = slice(h * HALF + q * LANES, h * HALF + (q + 1) * LANES)
                update = code[:, q * LANES:(q + 1) * LANES] * scale
                fresh = 0.9 * momentum_ref[b, :, at] + update
                new[b, :, at] = fresh
                direction[b, :, at] = (update + 0.9 * fresh).astype(BF16)
        if (b + 1) % STEP == 0:
            part = pl.ds(b + 1 - STEP, STEP)
            for n, (have, give) in enumerate(((new, new_hbm), (direction, direction_hbm))):
                copies.append(pltpu.make_async_copy(have.at[part], give.at[part], sem.at[n, b // STEP]))
                copies[-1].start()
    for copy in copies:
        copy.wait()


def apply_update(owner, back, head, momentum):
    return pl.pallas_call(
        update_kernel,
        out_shape=(
            jax.ShapeDtypeStruct((PAIRS, ROWS, B), F32),
            jax.ShapeDtypeStruct((PAIRS, ROWS, B), BF16),
        ),
        in_specs=[
            pl.BlockSpec(memory_space=pl.ANY),
            pl.BlockSpec(memory_space=pltpu.VMEM),
            pl.BlockSpec(memory_space=pltpu.VMEM),
            pl.BlockSpec(memory_space=pltpu.VMEM),
        ],
        out_specs=[pl.BlockSpec(memory_space=pltpu.HBM)] * 2,
        scratch_shapes=[
            pltpu.SMEM((1, PAIRS), jnp.int32),
            pltpu.VMEM((PAIRS, ROWS, B), F32),
            pltpu.VMEM((PAIRS, ROWS, B), BF16),
            pltpu.VMEM((PAIRS, ROWS, LANES), F32),
            pltpu.SemaphoreType.DMA,
            pltpu.SemaphoreType.DMA((2, PAIRS // STEP)),
        ],
        compiler_params=pltpu.CompilerParams(vmem_limit_bytes=24 * 1024 * 1024),
        name="update",
    )(owner, back, head, momentum)


def per_device(grads, momentum, root_factors, owner_table):
    factor = root_factors.reshape(Z, Y, 2, ROWS, B)
    back, head = exchange(owner_table, grads[0], factor)
    new_momentum, direction = apply_update(owner_table, back, head, momentum[0])
    return (new_momentum[None], direction[None])


def solution(mesh):
    in_specs = (
        P("mp", None, "dp", None),
        P("mp", None, "dp", None),
        P("mp", "dp", None, None),
        P("mp", None),
    )
    out_specs = (P("mp", None, "dp", None), P("mp", None, "dp", None))
    return jax.shard_map(
        per_device, mesh=mesh, in_specs=in_specs, out_specs=out_specs, check_vma=False
    )
```

```python
import jax
import jax.numpy as jnp
from jax import lax
from jax.experimental import pallas as pl
from jax.experimental.pallas import tpu as pltpu
from jax.sharding import PartitionSpec as P

Z, Y, X = 8, 4, 4
PAIRS = Z * Y
ROWS = 16
B = 1024
HALF = B // 2
LANES = 128
TOP = 32767.0
MESH = pl.DeviceIdType.MESH
F32 = jnp.float32
BF16 = jnp.bfloat16
OFFSETS = (4, 0, 2, 6, 3, 5, 1, 7)
OWN = OFFSETS.index(0)
PACKED = 6
HELD = PAIRS - 2 * Y


def offset_at(i):
    found = jnp.int32(OFFSETS[0])
    for n in range(1, Z):
        found = jnp.where(i == n, OFFSETS[n], found)
    return found


def packed_inverse(owner_row):
    lane = lax.broadcasted_iota(jnp.int32, (1, PAIRS), 1)
    words = []
    for w in range((PAIRS + PACKED - 1) // PACKED):
        at = owner_row - PACKED * w
        inside = (at >= 0) & (at < PACKED)
        shift = 5 * jnp.where(inside, at, 0)
        words.append(jnp.sum(jnp.where(inside, lane << shift, 0)))
    return words


def exchange_kernel(
    owner_rows, grads_hbm, factor_hbm,
    back_ref, head_ref,
    grads_ref, inverse, factor, outgoing, gathered, left, right, left_other, product, coded, heads, sums, seen,
    grads_sem, factor_sem, grad_send, grad_recv, sib_send, sib_recv, fac_send, fac_recv,
    back_send, back_recv, sum_send, sum_recv, head_send, head_recv, local_sem, head_local,
):
    me = lax.axis_index("dp")
    x = lax.axis_index("mp")
    z = me // (2 * Y)
    y = (me // 2) % Y
    c = me % 2
    pair = me // 2
    sibling = {"dp": pair * 2 + (1 - c)}

    def chip(i, dy):
        return lax.rem(z + Z - OFFSETS[i], Z) * Y + lax.rem(y + dy, Y)

    grads_in = pltpu.make_async_copy(grads_hbm, grads_ref, grads_sem)
    grads_in.start()

    barrier = pltpu.get_barrier_semaphore()

    partners = [(i, dy) for i in range(Z) for dy in range(Y) if (OFFSETS[i], dy) != (0, 0)]
    for i, dy in partners:
        pl.semaphore_signal(barrier, inc=1, device_id={"dp": chip(i, dy) * 2 + c}, device_id_type=MESH)

    pl.semaphore_signal(barrier, inc=1, device_id=sibling, device_id_type=MESH)

    @pl.loop(2, 2 * X)
    def _(s):
        target = {"dp": pair * 2 + lax.rem(c + s, 2), "mp": lax.rem(x + s // 2, X)}
        pl.semaphore_signal(barrier, inc=1, device_id=target, device_id_type=MESH)

    factor_in = pltpu.make_async_copy(factor_hbm, factor, factor_sem)
    factor_in.start()

    words = packed_inverse(owner_rows[...])
    for w, word in enumerate(words):
        inverse[w] = word
    grads_in.wait()
    for k in range(PAIRS):
        outgoing[k] = grads_ref[(words[k // PACKED] >> (5 * (k % PACKED))) & (PAIRS - 1)]

    pl.semaphore_wait(barrier, (PAIRS - 1) + 1 + (2 * X - 2))

    def send_rows(first):
        early = [p for p in partners if (OFFSETS[p[0]] + (1) * p[1] + first) % 2 == 0]
        late = [p for p in partners if p not in early]
        for i, dy in early + late:
            k = chip(i, dy)
            pltpu.make_async_remote_copy(
                src_ref=outgoing.at[k], dst_ref=gathered.at[i, y, c],
                send_sem=grad_send, recv_sem=grad_recv.at[i, y],
                device_id={"dp": k * 2 + c}, device_id_type=MESH,
            ).start()

    colour = (z + 1 * y) % 2
    for first in range(2):
        @pl.when(colour == first)
        def _(first=first):
            send_rows(first)

    own_rows = pltpu.make_async_copy(outgoing.at[pair], gathered.at[OWN, y, c], local_sem)
    own_rows.start()

    factor_in.wait()

    def split(part_ref, at, value):
        high = value.astype(BF16)
        part_ref[(0,) + at] = high
        part_ref[(1,) + at] = (value - high.astype(F32)).astype(BF16)

    @pl.when(c == 0)
    def _():
        @pl.loop(0, Z)
        def _(i):
            zi = lax.rem(z + offset_at(i), Z)
            for j in range(Z):
                zj = lax.rem(z + OFFSETS[j], Z)
                cols = pl.ds(pl.multiple_of(zj * LANES, LANES), LANES)
                to = pl.ds(j * LANES, LANES)
                split(left, (i, slice(None), slice(None), to), factor[zi, :, 0, :, cols])
                split(left_other, (i, slice(None), slice(None), to), factor[zi, :, 1, :, cols])
            pltpu.make_async_remote_copy(
                src_ref=left_other.at[:, i], dst_ref=left.at[:, i],
                send_sem=fac_send, recv_sem=fac_recv,
                device_id=sibling, device_id_type=MESH,
            ).start()

    @pl.when(c == 1)
    def _():
        @pl.loop(0, Z)
        def _(i):
            for q in range(Y):
                for h in range(2):
                    split(right, (i, q, h), factor[i, q, h])
            pltpu.make_async_remote_copy(
                src_ref=right.at[:, i], dst_ref=right.at[:, i],
                send_sem=fac_send, recv_sem=fac_recv,
                device_id=sibling, device_id_type=MESH,
            ).start()

    def whole(ref, send, recv):
        return pltpu.make_async_remote_copy(
            src_ref=ref, dst_ref=ref, send_sem=send, recv_sem=recv,
            device_id=sibling, device_id_type=MESH,
        )

    own_rows.wait()

    def arrived(i, dy):
        if (OFFSETS[i], dy) != (0, 0):
            q = lax.rem(y + dy, Y)
            whole(gathered.at[i, q, 0], grad_send, grad_recv.at[i, q]).wait_recv()

    def pass_on(part, i):
        pltpu.make_async_remote_copy(
            src_ref=part, dst_ref=part, send_sem=sib_send, recv_sem=sib_recv.at[i],
            device_id=sibling, device_id_type=MESH,
        ).start()

    def pass_on_two(j):
        if j < Y - 1:
            for i in (2 * j, 2 * j + 1):
                for dy in range(Y):
                    arrived(i, dy)
                pass_on(gathered.at[i, :, c], i)
        else:
            for dy in (0, 1, 3, 2):
                for i in (2 * j, 2 * j + 1):
                    arrived(i, dy)
                    pass_on(gathered.at[i, lax.rem(y + dy, Y), c], i)

    pass_on_two(0)

    @pl.when(c == 0)
    def _():
        whole(right, fac_send, fac_recv).wait_recv()

    @pl.when(c == 1)
    def _():
        whole(left, fac_send, fac_recv).wait_recv()

    for j in range(Y):
        if j > 0:
            pass_on_two(j)
        whole(gathered.at[2 * j, :, 0], sib_send, sib_recv.at[2 * j]).wait_recv()
        whole(gathered.at[2 * j + 1, :, 0], sib_send, sib_recv.at[2 * j + 1]).wait_recv()
        some = gathered[2 * j:2 * j + 2].reshape(2 * LANES, B)
        rows = left[:, :, :, :, j * 2 * LANES:(j + 1) * 2 * LANES].reshape(B, 2 * LANES)
        term = jnp.dot(rows, some, preferred_element_type=F32)
        term = term[:HALF] + term[HALF:]
        if j == 0:
            product[...] = term
        else:
            product[...] += term

    seen[...] = jnp.zeros_like(seen)
    lane = lax.broadcasted_iota(jnp.int32, (ROWS, LANES), 1)
    diagonal = lane == lax.broadcasted_iota(jnp.int32, (ROWS, LANES), 0)

    def partner(s):
        return lax.rem(z + offset_at(s // Y), Z) * Y + s % Y

    def give_back(s):
        k = partner(s)

        @pl.when(k != pair)
        def _():
            pltpu.make_async_remote_copy(
                src_ref=coded.at[s], dst_ref=back_ref.at[pair],
                send_sem=back_send, recv_sem=back_recv,
                device_id={"dp": k * 2 + c}, device_id_type=MESH,
            ).start()

        @pl.when(k == pair)
        def _():
            pltpu.make_async_copy(coded.at[s], back_ref.at[pair], local_sem).start()

    @pl.loop(0, Y)
    def _(j):
        base = pl.multiple_of(j * LANES, LANES)
        rows = product[pl.ds(base, LANES)]
        high = rows.astype(BF16)
        low = (rows - high.astype(F32)).astype(BF16)
        both = jnp.concatenate([high, low], axis=0)
        by_high = jnp.dot(both, right[0].reshape(B, B), preferred_element_type=F32)
        by_low = jnp.dot(high, right[1].reshape(B, B), preferred_element_type=F32)
        product[pl.ds(base, LANES)] = by_high[:LANES] + (by_high[LANES:] + by_low)

        @pl.loop(0, 2 * Y)
        def _(q):
            s = j * 2 * Y + q
            value = product[pl.ds(pl.multiple_of(s * ROWS, ROWS), ROWS)]
            seen[...] += _fold(value * value)
            size = jnp.abs(value)
            top = jnp.maximum(jnp.max(size, axis=1, keepdims=True), 1e-37)
            heads[s, 0:1] = jnp.sum(jnp.where(diagonal, jnp.broadcast_to(top, (ROWS, LANES)), 0.0), axis=0, keepdims=True)
            code = (jnp.sqrt(size * (1.0 / top)) * TOP + 0.5).astype(jnp.int32)
            code = jnp.where(value < 0.0, -code, code)
            coded[s] = (code[:, :HALF] & 0xFFFF) | (code[:, HALF:] << 16)

            @pl.when(s < HELD)
            def _():
                give_back(s)

    block = (inverse[pair // PACKED] >> (5 * (pair % PACKED))) & (PAIRS - 1)

    def grad_sum(i, total):
        rows = gathered[i, :, pl.ds(c, 1)].reshape(Y * ROWS, B).astype(F32)
        return total + _fold(rows * rows)

    grad_sq = jnp.sum(lax.fori_loop(0, Z, grad_sum, jnp.zeros((8, LANES), F32)))
    pre_sq = jnp.sum(seen[...])
    one = lax.broadcasted_iota(jnp.int32, (1, LANES), 1)
    sums[0] = jnp.where(one == block, pre_sq, 0.0) + jnp.where(one == block + 64, grad_sq, 0.0)

    @pl.loop(1, 2 * X)
    def _(s):
        target = {"dp": pair * 2 + lax.rem(c + s, 2), "mp": lax.rem(x + s // 2, X)}
        pltpu.make_async_remote_copy(
            src_ref=sums.at[0], dst_ref=sums.at[s],
            send_sem=sum_send, recv_sem=sum_recv,
            device_id=target, device_id_type=MESH,
        ).start()

    whole(sums.at[pl.ds(1, 2 * X - 1)], sum_send, sum_recv).wait()
    total = jnp.sum(sums[...], axis=0)

    @pl.loop(0, PAIRS)
    def _(s):
        heads[s, 1:2] = total
        k = partner(s)

        @pl.when(k != pair)
        def _():
            pltpu.make_async_remote_copy(
                src_ref=heads.at[s], dst_ref=head_ref.at[pair],
                send_sem=head_send, recv_sem=head_recv,
                device_id={"dp": k * 2 + c}, device_id_type=MESH,
            ).start()

        @pl.when(k == pair)
        def _():
            pltpu.make_async_copy(heads.at[s], head_ref.at[pair], head_local).start()

    @pl.loop(HELD, PAIRS)
    def _(s):
        give_back(s)

    others = pl.ds(0, PAIRS - 1)
    whole(outgoing.at[others], grad_send, grad_recv.at[0, 0]).wait_send()
    whole(gathered.at[:, :, 0], sib_send, sib_recv.at[0]).wait_send()

    @pl.when(c == 0)
    def _():
        whole(left_other, fac_send, fac_recv).wait_send()

    @pl.when(c == 1)
    def _():
        whole(right, fac_send, fac_recv).wait_send()

    pltpu.make_async_copy(coded.at[0], back_ref.at[pair], local_sem).wait()
    pltpu.make_async_copy(heads.at[0], head_ref.at[pair], head_local).wait()
    whole(back_ref.at[others], back_send, back_recv).wait()
    whole(head_ref.at[others], head_send, head_recv).wait()


def _fold(value):
    total = jnp.zeros((8, LANES), F32)
    for r in range(0, value.shape[0], 8):
        for q in range(0, value.shape[1], LANES):
            total = total + value[r:r + 8, q:q + LANES]
    return total


def exchange(owner, grads, factor):
    grads_words = (PAIRS, ROWS, B)
    return pl.pallas_call(
        exchange_kernel,
        out_shape=(
            jax.ShapeDtypeStruct((PAIRS, ROWS, HALF), jnp.int32),
            jax.ShapeDtypeStruct((PAIRS, 2, LANES), F32),
        ),
        in_specs=[
            pl.BlockSpec(memory_space=pltpu.VMEM),
            pl.BlockSpec(memory_space=pltpu.HBM),
            pl.BlockSpec(memory_space=pltpu.HBM),
        ],
        out_specs=[pl.BlockSpec(memory_space=pltpu.VMEM)] * 2,
        scratch_shapes=[
            pltpu.VMEM(grads_words, BF16),
            pltpu.SMEM((PACKED,), jnp.int32),
            pltpu.VMEM((Z, Y, 2, ROWS, B), F32),
            pltpu.VMEM(grads_words, BF16),
            pltpu.VMEM((Z, Y, 2, ROWS, B), BF16),
            pltpu.VMEM((2, Z, Y, ROWS, B), BF16),
            pltpu.VMEM((2, Z, Y, 2, ROWS, B), BF16),
            pltpu.VMEM((2, Z, Y, ROWS, B), BF16),
            pltpu.VMEM((HALF, B), F32),
            pltpu.VMEM((PAIRS, ROWS, HALF), jnp.int32),
            pltpu.VMEM((PAIRS, 2, LANES), F32),
            pltpu.VMEM((2 * X, 1, LANES), F32),
            pltpu.VMEM((8, LANES), F32),
            pltpu.SemaphoreType.DMA,
            pltpu.SemaphoreType.DMA,
            pltpu.SemaphoreType.DMA,
            pltpu.SemaphoreType.DMA((Z, Y)),
            pltpu.SemaphoreType.DMA,
            pltpu.SemaphoreType.DMA((Z,)),
            pltpu.SemaphoreType.DMA,
            pltpu.SemaphoreType.DMA,
            pltpu.SemaphoreType.DMA,
            pltpu.SemaphoreType.DMA,
            pltpu.SemaphoreType.DMA,
            pltpu.SemaphoreType.DMA,
            pltpu.SemaphoreType.DMA,
            pltpu.SemaphoreType.DMA,
            pltpu.SemaphoreType.DMA,
            pltpu.SemaphoreType.DMA,
        ],
        compiler_params=pltpu.CompilerParams(
            collective_id=0, has_side_effects=True, vmem_limit_bytes=52 * 1024 * 1024
        ),
        name="exchange",
    )(owner, grads, factor)


STEP = 4


def update_kernel(owner_in, back_ref, head_ref, momentum_ref, new_hbm, direction_hbm, owner_ref, new, direction, scales, owner_sem, sem):
    owner = pltpu.make_async_copy(owner_in, owner_ref, owner_sem)
    owner.start()
    lane = lax.broadcasted_iota(jnp.int32, (ROWS, LANES), 1)
    diagonal = lane == lax.broadcasted_iota(jnp.int32, (ROWS, LANES), 0)
    heads = head_ref[...]
    totals = jnp.sum(heads, axis=0)[1:2]
    grad = pltpu.roll(totals, 64, 1)
    graft = jnp.sqrt(grad) / (jnp.sqrt(totals) + 1e-06) * (1.0 / (TOP * TOP))
    for k in range(PAIRS):
        top = jnp.broadcast_to(heads[k, 0:1], (ROWS, LANES))
        top = jnp.sum(jnp.where(diagonal, top, 0.0), axis=1, keepdims=True)
        scales[k] = jnp.broadcast_to(top, (ROWS, LANES))
    owner.wait()
    copies = []
    for b in range(PAIRS):
        k = owner_ref[0, b]
        scale = scales[k] * jnp.broadcast_to(graft[:, b:b + 1], (ROWS, LANES))
        words = back_ref[k]
        for h, code in enumerate(((words << 16) >> 16, words >> 16)):
            code = code.astype(F32)
            code = code * jnp.abs(code)
            for q in range(HALF // LANES):
                at = slice(h * HALF + q * LANES, h * HALF + (q + 1) * LANES)
                update = code[:, q * LANES:(q + 1) * LANES] * scale
                fresh = 0.9 * momentum_ref[b, :, at] + update
                new[b, :, at] = fresh
                direction[b, :, at] = (update + 0.9 * fresh).astype(BF16)
        if (b + 1) % STEP == 0:
            part = pl.ds(b + 1 - STEP, STEP)
            for n, (have, give) in enumerate(((new, new_hbm), (direction, direction_hbm))):
                copies.append(pltpu.make_async_copy(have.at[part], give.at[part], sem.at[n, b // STEP]))
                copies[-1].start()
    for copy in copies:
        copy.wait()


def apply_update(owner, back, head, momentum):
    return pl.pallas_call(
        update_kernel,
        out_shape=(
            jax.ShapeDtypeStruct((PAIRS, ROWS, B), F32),
            jax.ShapeDtypeStruct((PAIRS, ROWS, B), BF16),
        ),
        in_specs=[
            pl.BlockSpec(memory_space=pl.ANY),
            pl.BlockSpec(memory_space=pltpu.VMEM),
            pl.BlockSpec(memory_space=pltpu.VMEM),
            pl.BlockSpec(memory_space=pltpu.VMEM),
        ],
        out_specs=[pl.BlockSpec(memory_space=pltpu.HBM)] * 2,
        scratch_shapes=[
            pltpu.SMEM((1, PAIRS), jnp.int32),
            pltpu.VMEM((PAIRS, ROWS, B), F32),
            pltpu.VMEM((PAIRS, ROWS, B), BF16),
            pltpu.VMEM((PAIRS, ROWS, LANES), F32),
            pltpu.SemaphoreType.DMA,
            pltpu.SemaphoreType.DMA((2, PAIRS // STEP)),
        ],
        compiler_params=pltpu.CompilerParams(vmem_limit_bytes=24 * 1024 * 1024),
        name="update",
    )(owner, back, head, momentum)


def per_device(grads, momentum, root_factors, owner_table):
    factor = root_factors.reshape(Z, Y, 2, ROWS, B)
    back, head = exchange(owner_table, grads[0], factor)
    new_momentum, direction = apply_update(owner_table, back, head, momentum[0])
    return (new_momentum[None], direction[None])


def solution(mesh):
    in_specs = (
        P("mp", None, "dp", None),
        P("mp", None, "dp", None),
        P("mp", "dp", None, None),
        P("mp", None),
    )
    out_specs = (P("mp", None, "dp", None), P("mp", None, "dp", None))
    return jax.shard_map(
        per_device, mesh=mesh, in_specs=in_specs, out_specs=out_specs, check_vma=False
    )
```

```python
import jax
import jax.numpy as jnp
from jax import lax
from jax.experimental import pallas as pl
from jax.experimental.pallas import tpu as pltpu
from jax.sharding import PartitionSpec as P

Z, Y, X = 8, 4, 4
PAIRS = Z * Y
ROWS = 16
B = 1024
HALF = B // 2
LANES = 128
TOP = 32767.0
MESH = pl.DeviceIdType.MESH
F32 = jnp.float32
BF16 = jnp.bfloat16
OFFSETS = (4, 0, 2, 6, 3, 5, 1, 7)
OWN = OFFSETS.index(0)
PACKED = 6
HELD = PAIRS - 9
CHUNKS = (128, 128, 128, 128)


def offset_at(i):
    found = jnp.int32(OFFSETS[0])
    for n in range(1, Z):
        found = jnp.where(i == n, OFFSETS[n], found)
    return found


def packed_inverse(owner_row):
    lane = lax.broadcasted_iota(jnp.int32, (1, PAIRS), 1)
    words = []
    for w in range((PAIRS + PACKED - 1) // PACKED):
        at = owner_row - PACKED * w
        inside = (at >= 0) & (at < PACKED)
        shift = 5 * jnp.where(inside, at, 0)
        words.append(jnp.sum(jnp.where(inside, lane << shift, 0)))
    return words


def exchange_kernel(
    owner_rows, grads_hbm, factor_hbm,
    rows_ref, scale_ref, sums_ref,
    owner_ref, back_ref, head_ref, grads_ref, inverse, factor, outgoing, gathered, left, right, left_other, product, coded, heads, sums, grad_seen,
    owner_sem, grads_sem, factor_sem, grad_send, grad_recv, sib_send, sib_recv, fac_send, fac_recv,
    back_send, back_recv, sum_send, sum_recv, head_send, head_recv, local_sem, head_local,
):
    me = lax.axis_index("dp")
    x = lax.axis_index("mp")
    z = me // (2 * Y)
    y = (me // 2) % Y
    c = me % 2
    pair = me // 2
    sibling = {"dp": pair * 2 + (1 - c)}

    def chip(i, dy):
        return lax.rem(z + Z - OFFSETS[i], Z) * Y + lax.rem(y + dy, Y)

    owner_in = pltpu.make_async_copy(owner_rows, owner_ref, owner_sem)
    owner_in.start()
    grads_in = pltpu.make_async_copy(grads_hbm, grads_ref, grads_sem)
    grads_in.start()

    barrier = pltpu.get_barrier_semaphore()

    partners = [(i, dy) for i in range(Z) for dy in range(Y) if (OFFSETS[i], dy) != (0, 0)]
    for i, dy in partners:
        pl.semaphore_signal(barrier, inc=1, device_id={"dp": chip(i, dy) * 2 + c}, device_id_type=MESH)

    pl.semaphore_signal(barrier, inc=1, device_id=sibling, device_id_type=MESH)

    @pl.loop(2, 2 * X)
    def _(s):
        target = {"dp": pair * 2 + lax.rem(c + s, 2), "mp": lax.rem(x + s // 2, X)}
        pl.semaphore_signal(barrier, inc=1, device_id=target, device_id_type=MESH)

    factor_in = pltpu.make_async_copy(factor_hbm, factor, factor_sem)
    factor_in.start()

    words = packed_inverse(owner_rows[...])
    for w, word in enumerate(words):
        inverse[w] = word
    grads_in.wait()
    for k in range(PAIRS):
        outgoing[k] = grads_ref[(words[k // PACKED] >> (5 * (k % PACKED))) & (PAIRS - 1)]

    pl.semaphore_wait(barrier, (PAIRS - 1) + 1 + (2 * X - 2))

    def by_turn(p):
        return (p[0] // 2, p[1], p[0])

    def send_rows(first):
        early = [p for p in partners if (OFFSETS[p[0]] + (1) * p[1] + first) % 2 == 0]
        late = [p for p in partners if p not in early]
        for i, dy in sorted(early, key=by_turn) + sorted(late, key=by_turn):
            k = chip(i, dy)
            pltpu.make_async_remote_copy(
                src_ref=outgoing.at[k], dst_ref=gathered.at[i, y, c],
                send_sem=grad_send, recv_sem=grad_recv.at[i, y],
                device_id={"dp": k * 2 + c}, device_id_type=MESH,
            ).start()

    colour = (z + 1 * y) % 2
    for first in range(2):
        @pl.when(colour == first)
        def _(first=first):
            send_rows(first)

    own_rows = pltpu.make_async_copy(outgoing.at[pair], gathered.at[OWN, y, c], local_sem)
    own_rows.start()

    factor_in.wait()

    def split(part_ref, at, value):
        high = value.astype(BF16)
        part_ref[(0,) + at] = high
        part_ref[(1,) + at] = (value - high.astype(F32)).astype(BF16)

    @pl.when(c == 0)
    def _():
        @pl.loop(0, Z)
        def _(i):
            zi = lax.rem(z + offset_at(i), Z)
            for j in range(Z):
                zj = lax.rem(z + OFFSETS[j], Z)
                cols = pl.ds(pl.multiple_of(zj * LANES, LANES), LANES)
                to = pl.ds(j * LANES, LANES)
                split(left, (i, slice(None), slice(None), to), factor[zi, :, 0, :, cols])
                split(left_other, (i, slice(None), slice(None), to), factor[zi, :, 1, :, cols])
            pltpu.make_async_remote_copy(
                src_ref=left_other.at[:, i], dst_ref=left.at[:, i],
                send_sem=fac_send, recv_sem=fac_recv,
                device_id=sibling, device_id_type=MESH,
            ).start()

    @pl.when(c == 1)
    def _():
        @pl.loop(0, Z)
        def _(i):
            for q in range(Y):
                for h in range(2):
                    split(right, (i, q, h), factor[i, q, h])
            pltpu.make_async_remote_copy(
                src_ref=right.at[:, i], dst_ref=right.at[:, i],
                send_sem=fac_send, recv_sem=fac_recv,
                device_id=sibling, device_id_type=MESH,
            ).start()

    def whole(ref, send, recv):
        return pltpu.make_async_remote_copy(
            src_ref=ref, dst_ref=ref, send_sem=send, recv_sem=recv,
            device_id=sibling, device_id_type=MESH,
        )

    own_rows.wait()

    def arrived(i, dy):
        if (OFFSETS[i], dy) != (0, 0):
            q = lax.rem(y + dy, Y)
            whole(gathered.at[i, q, 0], grad_send, grad_recv.at[i, q]).wait_recv()

    def pass_on(part, i):
        pltpu.make_async_remote_copy(
            src_ref=part, dst_ref=part, send_sem=sib_send, recv_sem=sib_recv.at[i],
            device_id=sibling, device_id_type=MESH,
        ).start()

    def pass_on_two(j):
        if j < Y - 1:
            for i in (2 * j, 2 * j + 1):
                for dy in range(Y):
                    arrived(i, dy)
                pass_on(gathered.at[i, :, c], i)
        else:
            for dy in (0, 1, 3, 2):
                for i in (2 * j, 2 * j + 1):
                    arrived(i, dy)
                    pass_on(gathered.at[i, lax.rem(y + dy, Y), c], i)

    pass_on_two(0)

    @pl.when(c == 0)
    def _():
        whole(right, fac_send, fac_recv).wait_recv()

    @pl.when(c == 1)
    def _():
        whole(left, fac_send, fac_recv).wait_recv()

    for j in range(Y):
        if j > 0:
            pass_on_two(j)
        whole(gathered.at[2 * j, :, 0], sib_send, sib_recv.at[2 * j]).wait_recv()
        whole(gathered.at[2 * j + 1, :, 0], sib_send, sib_recv.at[2 * j + 1]).wait_recv()
        some = gathered[2 * j:2 * j + 2].reshape(2 * LANES, B)
        rows = left[:, :, :, :, j * 2 * LANES:(j + 1) * 2 * LANES].reshape(B, 2 * LANES)
        term = jnp.dot(rows, some, preferred_element_type=F32)
        term = term[:HALF] + term[HALF:]
        if j == 0:
            product[...] = term
        else:
            product[...] += term
        own = gathered[2 * j:2 * j + 2, :, pl.ds(c, 1)].reshape(2 * Y * ROWS, B).astype(F32)
        squares = _fold(own * own)
        if j == 0:
            grad_seen[...] = squares
        else:
            grad_seen[...] += squares

    lane = lax.broadcasted_iota(jnp.int32, (ROWS, LANES), 1)
    diagonal = lane == lax.broadcasted_iota(jnp.int32, (ROWS, LANES), 0) + 2 * PAIRS

    def send_back(source, sent, landed, at_home, n):
        i, turn = n // (2 * Y) * 2 + n % 2, n % (2 * Y) // 2
        q = lax.rem(y + turn, Y)
        s = i * Y + q
        k = lax.rem(z + OFFSETS[i], Z) * Y + q
        if (i, turn) == (OWN, 0):
            pltpu.make_async_copy(source.at[s], landed.at[pair], at_home).start()
        else:
            pltpu.make_async_remote_copy(
                src_ref=source.at[s], dst_ref=landed.at[pair],
                send_sem=sent[0], recv_sem=sent[1],
                device_id={"dp": k * 2 + c}, device_id_type=MESH,
            ).start()

    def give_back(n):
        send_back(coded, (back_send, back_recv), back_ref, local_sem, n)

    def encode(s):
        value = product[pl.ds(pl.multiple_of(s * ROWS, ROWS), ROWS)]
        size = jnp.abs(value)
        top = jnp.maximum(jnp.max(size, axis=1, keepdims=True), 1e-37)
        heads[s] = jnp.sum(jnp.where(diagonal, jnp.broadcast_to(top, (ROWS, LANES)), 0.0), axis=0, keepdims=True)
        code = (jnp.sqrt(size * (1.0 / top)) * TOP + 0.5).astype(jnp.int32)
        code = jnp.where(value < 0.0, -code, code)
        coded[s] = (code[:, :HALF] & 0xFFFF) | (code[:, HALF:] << 16)

    def multiply(start, rows):
        part = product[start:start + rows]
        high = part.astype(BF16)
        low = (part - high.astype(F32)).astype(BF16)
        both = jnp.concatenate([high, low], axis=0)
        by_high = jnp.dot(both, right[0].reshape(B, B), preferred_element_type=F32)
        by_low = jnp.dot(high, right[1].reshape(B, B), preferred_element_type=F32)
        value = by_high[:rows] + (by_high[rows:] + by_low)
        product[start:start + rows] = value
        return _fold(value * value)

    def encode_all(start, rows):
        @pl.loop(0, rows // ROWS, unroll=4)
        def _(q):
            encode(start // ROWS + q)

    done = 0
    pre_tile = jnp.zeros((8, LANES), F32)
    for rows in CHUNKS:
        pre_tile = pre_tile + multiply(done, rows)
        if done + rows < HALF:
            encode_all(done, rows)
            for n in range(done // ROWS, min((done + rows) // ROWS, HELD)):
                give_back(n)
            done += rows

    owner_in.wait()

    block = (inverse[pair // PACKED] >> (5 * (pair % PACKED))) & (PAIRS - 1)
    grad_sq = jnp.sum(grad_seen[...])
    pre_sq = jnp.sum(pre_tile)
    one = lax.broadcasted_iota(jnp.int32, (1, LANES), 1)
    sums[0] = jnp.where(one == block, pre_sq, 0.0) + jnp.where(one == block + PAIRS, grad_sq, 0.0)
    for s in range(1, 2 * X):
        target = {"dp": pair * 2 + lax.rem(c + s, 2), "mp": lax.rem(x + s // 2, X)}
        pltpu.make_async_remote_copy(
            src_ref=sums.at[0], dst_ref=sums.at[s],
            send_sem=sum_send, recv_sem=sum_recv,
            device_id=target, device_id_type=MESH,
        ).start()
    encode_all(done, HALF - done)
    for n in range(done // ROWS, HELD):
        give_back(n)
    whole(sums.at[pl.ds(1, 2 * X - 1)], sum_send, sum_recv).wait()
    total = jnp.sum(sums[...], axis=0)
    heads[...] += total[None]
    for n in range(PAIRS):
        send_back(heads, (head_send, head_recv), head_ref, head_local, n)

    for n in range(HELD, PAIRS):
        give_back(n)

    others = pl.ds(0, PAIRS - 1)
    whole(outgoing.at[others], grad_send, grad_recv.at[0, 0]).wait_send()
    whole(gathered.at[:, :, 0], sib_send, sib_recv.at[0]).wait_send()

    @pl.when(c == 0)
    def _():
        whole(left_other, fac_send, fac_recv).wait_send()

    @pl.when(c == 1)
    def _():
        whole(right, fac_send, fac_recv).wait_send()

    pltpu.make_async_copy(coded.at[0], back_ref.at[pair], local_sem).wait()
    pltpu.make_async_copy(heads.at[0], head_ref.at[pair], head_local).wait()
    whole(back_ref.at[others], back_send, back_recv).wait()
    whole(head_ref.at[others], head_send, head_recv).wait()

    sums_ref[...] = jnp.sum(head_ref[...], axis=0)
    for b in range(PAIRS):
        k = owner_ref[0, b]
        rows_ref[b] = back_ref[k]
        scale_ref[b] = head_ref[k]


def _fold(value):
    total = jnp.zeros((8, LANES), F32)
    for r in range(0, value.shape[0], 8):
        for q in range(0, value.shape[1], LANES):
            total = total + value[r:r + 8, q:q + LANES]
    return total


def exchange(owner, grads, factor):
    grads_words = (PAIRS, ROWS, B)
    return pl.pallas_call(
        exchange_kernel,
        out_shape=(
            jax.ShapeDtypeStruct((PAIRS, ROWS, HALF), jnp.int32),
            jax.ShapeDtypeStruct((PAIRS, 1, LANES), F32),
            jax.ShapeDtypeStruct((1, LANES), F32),
        ),
        in_specs=[
            pl.BlockSpec(memory_space=pltpu.VMEM),
            pl.BlockSpec(memory_space=pltpu.HBM),
            pl.BlockSpec(memory_space=pltpu.HBM),
        ],
        out_specs=[pl.BlockSpec(memory_space=pltpu.VMEM)] * 3,
        scratch_shapes=[
            pltpu.SMEM((1, PAIRS), jnp.int32),
            pltpu.VMEM((PAIRS, ROWS, HALF), jnp.int32),
            pltpu.VMEM((PAIRS, 1, LANES), F32),
            pltpu.VMEM(grads_words, BF16),
            pltpu.SMEM((PACKED,), jnp.int32),
            pltpu.VMEM((Z, Y, 2, ROWS, B), F32),
            pltpu.VMEM(grads_words, BF16),
            pltpu.VMEM((Z, Y, 2, ROWS, B), BF16),
            pltpu.VMEM((2, Z, Y, ROWS, B), BF16),
            pltpu.VMEM((2, Z, Y, 2, ROWS, B), BF16),
            pltpu.VMEM((2, Z, Y, ROWS, B), BF16),
            pltpu.VMEM((HALF, B), F32),
            pltpu.VMEM((PAIRS, ROWS, HALF), jnp.int32),
            pltpu.VMEM((PAIRS, 1, LANES), F32),
            pltpu.VMEM((2 * X, 1, LANES), F32),
            pltpu.VMEM((8, LANES), F32),
            pltpu.SemaphoreType.DMA,
            pltpu.SemaphoreType.DMA,
            pltpu.SemaphoreType.DMA,
            pltpu.SemaphoreType.DMA,
            pltpu.SemaphoreType.DMA((Z, Y)),
            pltpu.SemaphoreType.DMA,
            pltpu.SemaphoreType.DMA((Z,)),
            pltpu.SemaphoreType.DMA,
            pltpu.SemaphoreType.DMA,
            pltpu.SemaphoreType.DMA,
            pltpu.SemaphoreType.DMA,
            pltpu.SemaphoreType.DMA,
            pltpu.SemaphoreType.DMA,
            pltpu.SemaphoreType.DMA,
            pltpu.SemaphoreType.DMA,
            pltpu.SemaphoreType.DMA,
            pltpu.SemaphoreType.DMA,
        ],
        compiler_params=pltpu.CompilerParams(
            collective_id=0, has_side_effects=True, vmem_limit_bytes=52 * 1024 * 1024
        ),
        name="exchange",
    )(owner, grads, factor)


STEP = 4


def update_kernel(rows_ref, scale_ref, sums_ref, momentum_ref, new_hbm, direction_hbm, new, direction, sem):
    lane = lax.broadcasted_iota(jnp.int32, (ROWS, LANES), 1)
    diagonal = lane == lax.broadcasted_iota(jnp.int32, (ROWS, LANES), 0) + 2 * PAIRS
    totals = sums_ref[...]
    grad = pltpu.roll(totals, LANES - PAIRS, 1)
    graft = jnp.sqrt(grad) / (jnp.sqrt(totals) + 1e-06) * (1.0 / (TOP * TOP))
    copies = []
    for b in range(PAIRS):
        top = jnp.where(diagonal, jnp.broadcast_to(scale_ref[b], (ROWS, LANES)), 0.0)
        top = jnp.sum(top, axis=1, keepdims=True)
        scale = jnp.broadcast_to(top, (ROWS, LANES)) * jnp.broadcast_to(graft[:, b:b + 1], (ROWS, LANES))
        words = rows_ref[b]
        for h, code in enumerate(((words << 16) >> 16, words >> 16)):
            code = code.astype(F32)
            code = code * jnp.abs(code)
            for q in range(HALF // LANES):
                at = slice(h * HALF + q * LANES, h * HALF + (q + 1) * LANES)
                update = code[:, q * LANES:(q + 1) * LANES] * scale
                fresh = 0.9 * momentum_ref[b, :, at] + update
                new[b, :, at] = fresh
                direction[b, :, at] = (update + 0.9 * fresh).astype(BF16)
        if (b + 1) % STEP == 0:
            part = pl.ds(b + 1 - STEP, STEP)
            for n, (have, give) in enumerate(((new, new_hbm), (direction, direction_hbm))):
                copies.append(pltpu.make_async_copy(have.at[part], give.at[part], sem.at[n, b // STEP]))
                copies[-1].start()
    for copy in copies:
        copy.wait()


def apply_update(rows, scale, sums, momentum):
    return pl.pallas_call(
        update_kernel,
        out_shape=(
            jax.ShapeDtypeStruct((PAIRS, ROWS, B), F32),
            jax.ShapeDtypeStruct((PAIRS, ROWS, B), BF16),
        ),
        in_specs=[
            pl.BlockSpec(memory_space=pltpu.VMEM),
            pl.BlockSpec(memory_space=pltpu.VMEM),
            pl.BlockSpec(memory_space=pltpu.VMEM),
            pl.BlockSpec(memory_space=pltpu.VMEM),
        ],
        out_specs=[pl.BlockSpec(memory_space=pltpu.HBM)] * 2,
        scratch_shapes=[
            pltpu.VMEM((PAIRS, ROWS, B), F32),
            pltpu.VMEM((PAIRS, ROWS, B), BF16),
            pltpu.SemaphoreType.DMA((2, PAIRS // STEP)),
        ],
        compiler_params=pltpu.CompilerParams(vmem_limit_bytes=24 * 1024 * 1024),
        name="update",
    )(rows, scale, sums, momentum)


def per_device(grads, momentum, root_factors, owner_table):
    factor = root_factors.reshape(Z, Y, 2, ROWS, B)
    rows, scale, sums = exchange(owner_table, grads[0], factor)
    new_momentum, direction = apply_update(rows, scale, sums, momentum[0])
    return (new_momentum[None], direction[None])


def solution(mesh):
    in_specs = (
        P("mp", None, "dp", None),
        P("mp", None, "dp", None),
        P("mp", "dp", None, None),
        P("mp", None),
    )
    out_specs = (P("mp", None, "dp", None), P("mp", None, "dp", None))
    return jax.shard_map(
        per_device, mesh=mesh, in_specs=in_specs, out_specs=out_specs, check_vma=False
    )
```
